512 devices in a mesh: dp: 16 (over y_lo, x, core), mp: 32 (over y_hi, z).
Axes of the slice: x: 4, y: 4 (y_hi: 2, y_lo: 2; y = y_hi * 2 + y_lo), z: 16, core: 2. Of those that a mesh axis runs over, the one named last changes fastest.
Arguments:
- hidden: bfloat16 [8192, 16384], P('dp', 'mp'), may hold values from -6 to 6
- out_grad: bfloat16 [8192, 4096], P('dp', 'mp'), may hold values from -0.125 to 0.125
- token_counts: int32 [16], P('dp'), may hold values from 1 to 512, 5120 in all
- factor_state: float32 [8192, 16384], P('dp', 'mp'), as said below
- stale_root: bfloat16 [8192, 16384], P('dp', 'mp'), as said below
- newton_steps: int32 [16, 32], P('dp', 'mp'), may hold values from 0 to 3, as said below
Outputs:
- update: bfloat16 [4096, 16384], P('dp', 'mp')
- new_factor: float32 [8192, 16384], P('dp', 'mp')
- new_root: bfloat16 [8192, 16384], P('dp', 'mp')
The draws below stay inside these ranges and needn't reach their ends.
Inputs may be any that keep to these rules, and one draw needn't show every extreme that they name: `token_counts`: the shards' counts sum to 5120; some shard is full. `factor_state`: every 512 x 512 block is symmetric with a strictly dominant positive diagonal. `stale_root`: every 512 x 512 block is symmetric with a strictly dominant positive diagonal. `newton_steps`: 0 keeps the stale root; a factor that is refreshed takes 2 or 3 iterations; some factor takes 3.
All inputs are finite; a program needn't handle non-finite values.
Results may differ from the reference program's by a relative error of at most 0.03.
Values may be sent and summed in bfloat16 or wider, within the bound.
No kernel may reach another device: no remote copies, remote signals or barrier semaphores. Data moves between devices by JAX's collectives and lax.ppermute only.
A program may use at most 64 MiB of HBM per device.

```python
import math
import jax
import jax.numpy as jnp
import numpy as np
from jax import lax

B = 512
NEWTON = 3
TOK_DEV = 512
TOKENS = 8192
FW = 16384
DW = 4096
N_DP = 16
N_MP = 32


def dominant_field(key, lowest, highest):
    first, second = jax.random.split(key)
    uniform_part = jax.random.uniform(first, (N_DP, B, N_MP, B), jnp.float32, -1.0, 1.0)
    shaped = jnp.sign(uniform_part) * jnp.abs(uniform_part)
    symmetric = 0.5 * (shaped + jnp.transpose(shaped, (0, 3, 2, 1)))
    diagonal_values = lowest * jnp.exp(jax.random.uniform(second, (N_DP, B, N_MP), jnp.float32) * jnp.log(highest / lowest))
    diagonal_mask = jnp.eye(B, dtype=jnp.float32)[None, :, None, :]
    field = lowest / B * symmetric * (1.0 - diagonal_mask) + diagonal_values[..., None] * diagonal_mask
    return field.reshape(N_DP * B, N_MP * B)


def draw_factor_state(key, part):
    key = jax.random.fold_in(key, 11)
    return dominant_field(key, 30.0, 300.0)


def draw_stale_root(key, part):
    key = jax.random.fold_in(key, 13)
    return dominant_field(key, 0.1, 0.3).astype(jnp.bfloat16)


def draw_newton_steps(key, part):
    key = jax.random.fold_in(key, 17)
    first, second = jax.random.split(key)
    pick = jax.random.randint(first, (N_DP * N_MP,), 0, 4)
    steps = jnp.where(pick == 0, 0, jnp.where(pick == 3, 3, 2))
    chosen = jax.random.randint(second, (), 0, N_DP * N_MP)
    steps = jnp.where(jnp.arange(N_DP * N_MP) == chosen, 3, steps)
    return steps.reshape(N_DP, N_MP).astype(jnp.int32)


def strengthened(array, stream_key, source, target, shards_of, factor):
    owner, partner = [(jnp.arange(array.shape[dim]) // (array.shape[dim] // shards_of)).reshape([-1 if axis == dim else 1 for axis in range(array.ndim)]) for dim in (source, target)]
    chosen = jax.random.permutation(stream_key, shards_of)[partner]
    strong = (owner == chosen) | (owner == (partner + shards_of // 2) % shards_of)
    return jnp.where(strong, factor * array, array)


def steps_of(rng, extent, cuts, low, top_value):
    loudness = 1.0
    for axis_at, shards_of in cuts:
        heights = jax.random.uniform(jax.random.fold_in(jax.random.fold_in(rng, 6), axis_at), (shards_of,), jnp.float32, low / len(cuts), top_value / len(cuts))
        loudness = loudness * jnp.repeat(jnp.exp(heights), extent[axis_at] // shards_of).reshape((-1,) + (1,) * (len(extent) - 1 - axis_at))
    return loudness


def split_up(number_of, total, reach, lean):
    portions = [(1 << 20) // math.isqrt(rank ** lean) + 1 for rank in range(2, number_of + 1)]
    surplus, holding = total - reach - (number_of - 1), [1] * (number_of - 1)
    while surplus > 0:
        free = [i for i in range(number_of - 1) if holding[i] < reach]
        whole, remaining = sum([portions[i] for i in free]), surplus
        for i in free:
            more = min(reach - holding[i], max(1, remaining * portions[i] // whole), surplus)
            holding[i] = holding[i] + more
            surplus = surplus - more
    return np.array([reach] + holding)


def uneven_parts(own_key, count, total, bound, skew):
    if count == 2:
        one = jax.random.randint(own_key, (), max(1, total - bound), min(bound, total - 1) + 1)
        return jnp.stack([one, total - one])
    sizes = jnp.asarray(split_up(count, total, bound, skew), jnp.int32)
    couples = (count - 1) // 2
    donor, taker = sizes[1:1 + 2 * couples:2], sizes[2:2 + 2 * couples:2]
    margin = jnp.minimum(donor - 1, bound - taker)
    shifted = jax.random.randint(jax.random.fold_in(own_key, 1), (couples,), 0, 1 << 20) % (margin + 1)
    sizes = sizes.at[1:1 + 2 * couples:2].set(donor - shifted).at[2:2 + 2 * couples:2].set(taker + shifted)
    return sizes[jax.random.permutation(jax.random.fold_in(own_key, 2), count)]


def bell_draw(own_key, dims, spread, limit, cuts=(), held_as=jnp.bfloat16):
    result = jax.random.normal(own_key, dims, jnp.float32) * spread
    if len(cuts) > 0:
        result = steps_of(own_key, dims, cuts, -0.22, 0.18) * result
    return jnp.clip(result, min=-limit, max=limit).astype(held_as)


def bell_draw_with(stream_key, extent, spread, limit, cuts, heavy, kind=jnp.bfloat16):
    drawn = spread * jax.random.normal(stream_key, extent, jnp.float32)
    if cuts:
        drawn = drawn * steps_of(stream_key, extent, cuts, -0.22, 0.18)
    return jnp.clip(strengthened(drawn, jax.random.fold_in(stream_key, 3), *heavy), -limit, limit).astype(kind)


def setup_inputs(seed: int = 0) -> dict:
    arg_keys = jax.random.split(jax.random.key(seed), 7)
    hidden = bell_draw(arg_keys[0], (TOKENS, FW), 1.0, 6.0, ((0, 16), (1, 32)))
    out_grad = bell_draw_with(arg_keys[1], (TOKENS, DW), TOKENS ** -0.5, 0.125, ((0, 16), (1, 32)), (0, 1, 32, 2.75))
    token_counts = uneven_parts(arg_keys[2], N_DP, N_DP * TOK_DEV * 5 // 8, TOK_DEV, 2).astype(jnp.int32)
    factor_state = draw_factor_state(jax.random.fold_in(arg_keys[6], 71), 0)
    stale_root = draw_stale_root(jax.random.fold_in(arg_keys[6], 71), 0)
    newton_steps = draw_newton_steps(jax.random.fold_in(arg_keys[6], 71), 0)
    return {"hidden": hidden, "out_grad": out_grad, "token_counts": token_counts, "factor_state": factor_state, "stale_root": stale_root, "newton_steps": newton_steps}


BETA = 0.9
NORM_EPS = 1e-06

def newton_turn(matrix):
    identity = jnp.eye(matrix.shape[0], dtype=jnp.float32)
    return ((5.0 * identity - matrix.astype(jnp.float32)) * 0.25).astype(jnp.bfloat16)

def coupled_root(start, root_scale, steps):
    turned = newton_turn(start)
    current = (root_scale * turned.astype(jnp.float32)).astype(jnp.bfloat16)
    state = (current, start, turned)
    for level in range(1, NEWTON):

        def advance(carried):
            current, matrix, turned = carried
            square = jnp.dot(turned, turned, preferred_element_type=jnp.float32).astype(jnp.bfloat16)
            fourth = jnp.dot(square, square, preferred_element_type=jnp.float32).astype(jnp.bfloat16)
            matrix = jnp.dot(fourth, matrix, preferred_element_type=jnp.float32).astype(jnp.bfloat16)
            turned = newton_turn(matrix)
            current = jnp.dot(current, turned, preferred_element_type=jnp.float32).astype(jnp.bfloat16)
            return (current, matrix, turned)

        def keep(carried):
            return carried
        state = lax.cond(level < steps, advance, keep, state)
    return state[0]

def reference(hidden, out_grad, token_counts, factor_state, stale_root, newton_steps):
    token_index = jnp.arange(TOKENS, dtype=jnp.int32)
    positions = token_index % TOK_DEV
    limits = token_counts[token_index // TOK_DEV]
    kept = jnp.where((positions < limits)[:, None], hidden, jnp.zeros_like(hidden))

    def add_shard(total, index):
        hidden_rows = lax.dynamic_slice_in_dim(kept, index * TOK_DEV, TOK_DEV, 0)
        grad_rows = lax.dynamic_slice_in_dim(out_grad, index * TOK_DEV, TOK_DEV, 0)
        term = lax.dot_general(grad_rows, hidden_rows, (((0,), (0,)), ((), ())), preferred_element_type=jnp.float32)
        rounded = lax.optimization_barrier(term.astype(jnp.bfloat16))
        return (total + rounded.astype(jnp.float32), None)
    summed, _ = lax.scan(add_shard, jnp.zeros((DW, FW), jnp.float32), jnp.arange(N_DP, dtype=jnp.int32))
    grad = summed.astype(jnp.bfloat16)

    def one_block(index):
        row_block = index // N_MP
        col_block = index % N_MP
        grad_block = lax.dynamic_slice(grad, (row_block * B, col_block * B), (B, B))
        factors = []
        roots = []
        for side in range(2):
            operand = grad_block if side == 0 else grad_block.T
            statistic = lax.dot_general(operand, operand, (((1,), (1,)), ((), ())), preferred_element_type=jnp.float32)
            anchor = ((2 * row_block + side) * B, col_block * B)
            previous = lax.dynamic_slice(factor_state, anchor, (B, B))
            fresh = BETA * previous + (1.0 - BETA) * statistic
            norm_value = jnp.sqrt(jnp.sum(fresh * fresh) + NORM_EPS)
            scaled = (fresh / norm_value).astype(jnp.bfloat16)
            root_scale = (norm_value ** (-0.25)).astype(jnp.bfloat16)
            steps = newton_steps[2 * row_block + side, col_block]
            stale = lax.dynamic_slice(stale_root, anchor, (B, B))
            iterate = coupled_root(scaled, root_scale.astype(jnp.float32), steps)
            factors.append(fresh)
            roots.append(jnp.where(steps > 0, iterate, stale))
        product = jnp.dot(grad_block, roots[1], preferred_element_type=jnp.float32).astype(jnp.bfloat16)
        raw_update = jnp.dot(roots[0], product, preferred_element_type=jnp.float32)
        grad_square = jnp.sum(jnp.square(grad_block.astype(jnp.float32)))
        ratio = jnp.sqrt(grad_square) / jnp.sqrt(jnp.sum(raw_update * raw_update) + NORM_EPS)
        return ((raw_update * ratio).astype(jnp.bfloat16), jnp.stack(factors), jnp.stack(roots))
    blocks_all = N_DP // 2 * N_MP
    updates, factors, roots = lax.map(one_block, jnp.arange(blocks_all, dtype=jnp.int32))
    update = updates.reshape(N_DP // 2, N_MP, B, B).transpose(0, 2, 1, 3).reshape(DW, FW)
    new_factor = factors.reshape(N_DP // 2, N_MP, 2, B, B).transpose(0, 2, 3, 1, 4).reshape(N_DP * B, N_MP * B)
    new_root = roots.reshape(N_DP // 2, N_MP, 2, B, B).transpose(0, 2, 3, 1, 4).reshape(N_DP * B, N_MP * B)
    return (update, new_factor, new_root)
```

```python
import functools

import jax
import jax.numpy as jnp
from jax import lax
from jax.experimental import pallas as pl
from jax.experimental.pallas import tpu as pltpu
from jax.sharding import Mesh
from jax.sharding import PartitionSpec as P

BETA = 0.9
NORM_EPS = 1e-06
BLOCK = 512
HALF = BLOCK // 2
CLASSES = 4
VMEM = pl.BlockSpec(memory_space=pltpu.VMEM)
SMEM = pl.BlockSpec(memory_space=pltpu.SMEM)
LIMIT = pltpu.CompilerParams(vmem_limit_bytes=48 * 2**20)
AXES = ("y_lo", "x", "core", "y_hi", "z")
BF16 = jnp.bfloat16
F32 = jnp.float32


def dot(a, b, contract=((1,), (0,))):
    return lax.dot_general(a, b, (contract, ((), ())), preferred_element_type=F32)


def partial_kernel(classes, *refs):
    features, hidden, out = refs[:classes], refs[classes:-1], refs[-1]
    rows = features[0].shape[0] // CLASSES
    tokens = hidden[0].shape[0]
    for column in range(2):
        for at in range(classes):
            total = dot(features[at][:, :tokens], hidden[2 * column][...])
            total += dot(features[at][:, tokens:], hidden[2 * column + 1][...])
            total = total.astype(BF16)
            for block in range(CLASSES):
                out[column * CLASSES + block, at * rows : (at + 1) * rows, :] = total[
                    block * rows : (block + 1) * rows
                ]


def partials(features, hidden):
    classes = len(features)
    rows = features[0].shape[0] // CLASSES
    width = hidden[0].shape[1]
    return pl.pallas_call(
        functools.partial(partial_kernel, classes),
        out_shape=jax.ShapeDtypeStruct((2 * CLASSES, classes * rows, width), BF16),
        in_specs=[VMEM] * (classes + 4),
        out_specs=VMEM,
        compiler_params=LIMIT,
    )(*features, *hidden)


def newton_kernel(info, own, other, state, stale, new_factor, new_root, payload, grad_square, grad, matrix, turned, square):
    side, first, steps = info[0], info[1], info[2]
    rows = HALF // CLASSES
    for at, shift in enumerate((0, 1, 3, 2)):
        start = lax.rem(first + shift, CLASSES) * (2 * rows)
        mine = pl.multiple_of(start + side * rows, rows)
        theirs = pl.multiple_of(start + (1 - side) * rows, rows)
        grad[pl.ds(mine, rows), :] = own[at * rows : (at + 1) * rows, :]
        grad[pl.ds(theirs, rows), :] = other[at * rows : (at + 1) * rows, :]

    @pl.when(side == 0)
    def _():
        new_factor[...] = BETA * state[...] + (1.0 - BETA) * dot(grad[...], grad[...], ((1,), (1,)))

    @pl.when(side != 0)
    def _():
        new_factor[...] = BETA * state[...] + (1.0 - BETA) * dot(grad[...], grad[...], ((0,), (0,)))

    grad_square[...] = jnp.sum(jnp.square(grad[...].astype(F32)), keepdims=True)
    new_root[...] = stale[...]

    def turn(value):
        row = lax.broadcasted_iota(jnp.int32, value.shape, 0)
        column = lax.broadcasted_iota(jnp.int32, value.shape, 1)
        identity = jnp.where(row == column, 5.0, 0.0)
        return ((identity - value.astype(F32)) * 0.25).astype(BF16)

    @pl.when(steps > 0)
    def _():
        factor = new_factor[...]
        norm = jnp.sqrt(jnp.sum(factor * factor, keepdims=True) + NORM_EPS)
        matrix[...] = (factor * (1.0 / norm)).astype(BF16)
        root_scale = lax.rsqrt(jnp.sqrt(norm)).astype(BF16).astype(F32)
        turned[...] = turn(matrix[...])
        new_root[...] = (root_scale * turned[...].astype(F32)).astype(BF16)

        def advance(level, carry):
            square[...] = dot(turned[...], turned[...]).astype(BF16)
            square[...] = dot(square[...], square[...]).astype(BF16)
            matrix[...] = dot(square[...], matrix[...]).astype(BF16)
            turned[...] = turn(matrix[...])
            new_root[...] = dot(new_root[...], turned[...]).astype(BF16)
            return carry

        lax.fori_loop(1, steps, advance, 0)

    @pl.when(side == 0)
    def _():
        payload[...] = new_root[...]

    @pl.when(side != 0)
    def _():
        payload[...] = dot(grad[...], new_root[...]).astype(BF16)


def roots(info, own, other, state, stale):
    full = jax.ShapeDtypeStruct((BLOCK, BLOCK), BF16)
    return pl.pallas_call(
        newton_kernel,
        out_shape=(
            jax.ShapeDtypeStruct((BLOCK, BLOCK), F32),
            full,
            full,
            jax.ShapeDtypeStruct((1, 1), F32),
        ),
        in_specs=[SMEM] + [VMEM] * 4,
        out_specs=[VMEM] * 4,
        scratch_shapes=[pltpu.VMEM((BLOCK, BLOCK), BF16)] * 4,
        compiler_params=LIMIT,
    )(info, own, other, state, stale)


def update_kernel(info, own, other, grad_square, out):
    side = info[0]

    def finish(left, product, start):
        raw = dot(left[...], product[...])
        total = jnp.sum(raw * raw, keepdims=True)
        ratio = jnp.sqrt(grad_square[...]) / jnp.sqrt(total + NORM_EPS)
        out[...] = (raw[start : start + HALF] * ratio).astype(BF16)

    @pl.when(side == 0)
    def _():
        finish(own, other, 0)

    @pl.when(side != 0)
    def _():
        finish(other, own, HALF)


def grafted(info, own, other, grad_square):
    return pl.pallas_call(
        update_kernel,
        out_shape=jax.ShapeDtypeStruct((HALF, BLOCK), BF16),
        in_specs=[SMEM] + [VMEM] * 3,
        out_specs=VMEM,
        compiler_params=LIMIT,
    )(info, own, other, grad_square)


def other_of(value, axis):
    return lax.ppermute(value, axis, [(0, 1), (1, 0)])


def along_z(value, by):
    size = lax.axis_size("z")
    return lax.ppermute(value, "z", [(i, (i - by) % size) for i in range(size)])


def two_away(value):
    size = lax.axis_size("z")
    pairs = [(i, (i - 2) % size) for i in range(size)]
    pairs += [(size + i, size + (i + 2) % size) for i in range(size)]
    return lax.ppermute(value, ("core", "z"), pairs)


def to_home(value):
    pairs = [(2 * lo + hi, 2 * hi + (hi ^ lo)) for lo in range(2) for hi in range(2)]
    return lax.ppermute(value, ("y_lo", "y_hi"), pairs)


def reduced(parts):
    got = lax.all_to_all(parts, ("y_lo", "x"), 0, 0, tiled=True)
    return jnp.sum(got.astype(F32), axis=0).astype(BF16)


def per_device(hidden, out_grad, token_counts, factor_state, stale_root, newton_steps):
    core = lax.axis_index("core")
    first = lax.rem(lax.axis_index("z"), CLASSES)
    far = other_of(hidden, "y_hi")
    near = other_of(hidden, "core")
    positions = lax.broadcasted_iota(jnp.int32, (out_grad.shape[0], 1), 0)
    kept = jnp.where(positions < token_counts[0], out_grad, jnp.zeros_like(out_grad)).T
    rows = kept.shape[0] // 2
    mine = lax.dynamic_slice_in_dim(kept, core * rows, rows, 0)
    sent = lax.dynamic_slice_in_dim(kept, (1 - core) * rows, rows, 0)
    block = jnp.concatenate([mine, other_of(sent, "core")], axis=1)
    size = lax.axis_size("z")
    strided = [[at + CLASSES * i for i in range(size // CLASSES)] for at in range(CLASSES)]
    own_class = lax.all_gather(block, "z", axis=0, tiled=True, axis_index_groups=strided)
    above = along_z(own_class, 1)
    below = along_z(own_class, -1)
    across = two_away(own_class)
    columns = (hidden, near, far, other_of(far, "core"))
    pieces = [
        reduced(partials([own_class], columns)),
        reduced(partials([above, below], columns)),
        reduced(partials([across], columns)),
    ]
    own = to_home(jnp.concatenate(pieces, axis=0))
    other = other_of(own, "core")
    info = jnp.stack([core, first, newton_steps[0, 0]]).astype(jnp.int32)
    new_factor, new_root, payload, grad_square = roots(info, own, other, factor_state, stale_root)
    update = grafted(info, payload, other_of(payload, "core"), grad_square)
    return (update, new_factor, new_root)


def solution(mesh):
    fine = Mesh(mesh.devices.reshape(2, 4, 2, 2, 16), AXES)
    spec = P(AXES[:3], AXES[3:])
    in_specs = (spec, spec, P(AXES[:3]), spec, spec, spec)
    return jax.shard_map(per_device, mesh=fine, in_specs=in_specs, out_specs=(spec, spec, spec), check_vma=False)
```

```python
import functools

import jax
import jax.numpy as jnp
from jax import lax
from jax.experimental import pallas as pl
from jax.experimental.pallas import tpu as pltpu
from jax.sharding import Mesh
from jax.sharding import PartitionSpec as P

BETA = 0.9
NORM_EPS = 1e-06
BLOCK = 512
HALF = BLOCK // 2
CLASSES = 4
VMEM = pl.BlockSpec(memory_space=pltpu.VMEM)
SMEM = pl.BlockSpec(memory_space=pltpu.SMEM)
LIMIT = pltpu.CompilerParams(vmem_limit_bytes=48 * 2**20)
AXES = ("y_lo", "x", "core", "y_hi", "z")
BF16 = jnp.bfloat16
F32 = jnp.float32


def dot(a, b, contract=((1,), (0,))):
    return lax.dot_general(a, b, (contract, ((), ())), preferred_element_type=F32)


def partial_kernel(classes, *refs):
    features, hidden, out = refs[:classes], refs[classes:-1], refs[-1]
    rows = features[0].shape[0] // CLASSES
    tokens = hidden[0].shape[0]
    for column in range(2):
        for at in range(classes):
            total = dot(features[at][:, :tokens], hidden[2 * column][...])
            total += dot(features[at][:, tokens:], hidden[2 * column + 1][...])
            total = total.astype(BF16)
            for block in range(CLASSES):
                out[column * CLASSES + block, at * rows : (at + 1) * rows, :] = total[
                    block * rows : (block + 1) * rows
                ]


def partials(features, hidden):
    classes = len(features)
    rows = features[0].shape[0] // CLASSES
    width = hidden[0].shape[1]
    return pl.pallas_call(
        functools.partial(partial_kernel, classes),
        out_shape=jax.ShapeDtypeStruct((2 * CLASSES, classes * rows, width), BF16),
        in_specs=[VMEM] * (classes + 4),
        out_specs=VMEM,
        compiler_params=LIMIT,
    )(*features, *hidden)


def newton_kernel(info, own, last, other, other_last, state, stale, new_factor, new_root, payload, grad_square, grad, matrix, turned, square):
    side, first, steps = info[0], info[1], info[2]
    rows = HALF // CLASSES
    for at, shift in enumerate((0, 1, 3, 2)):
        start = lax.rem(first + shift, CLASSES) * (2 * rows)
        mine = pl.multiple_of(start + side * rows, rows)
        theirs = pl.multiple_of(start + (1 - side) * rows, rows)
        if at < CLASSES - 1:
            grad[pl.ds(mine, rows), :] = own[at * rows : (at + 1) * rows, :]
            grad[pl.ds(theirs, rows), :] = other[at * rows : (at + 1) * rows, :]
        else:
            grad[pl.ds(mine, rows), :] = last[...]
            grad[pl.ds(theirs, rows), :] = other_last[...]

    @pl.when(side == 0)
    def _():
        new_factor[...] = BETA * state[...] + (1.0 - BETA) * dot(grad[...], grad[...], ((1,), (1,)))

    @pl.when(side != 0)
    def _():
        new_factor[...] = BETA * state[...] + (1.0 - BETA) * dot(grad[...], grad[...], ((0,), (0,)))

    grad_square[...] = jnp.sum(jnp.square(grad[...].astype(F32)), keepdims=True)
    new_root[...] = stale[...]

    def turn(value):
        row = lax.broadcasted_iota(jnp.int32, value.shape, 0)
        column = lax.broadcasted_iota(jnp.int32, value.shape, 1)
        identity = jnp.where(row == column, 5.0, 0.0)
        return ((identity - value.astype(F32)) * 0.25).astype(BF16)

    @pl.when(steps > 0)
    def _():
        factor = new_factor[...]
        norm = jnp.sqrt(jnp.sum(factor * factor, keepdims=True) + NORM_EPS)
        matrix[...] = (factor * (1.0 / norm)).astype(BF16)
        root_scale = lax.rsqrt(jnp.sqrt(norm)).astype(BF16).astype(F32)
        turned[...] = turn(matrix[...])
        new_root[...] = (root_scale * turned[...].astype(F32)).astype(BF16)

        def advance(level, carry):
            square[...] = dot(turned[...], turned[...]).astype(BF16)
            square[...] = dot(square[...], square[...]).astype(BF16)
            matrix[...] = dot(square[...], matrix[...]).astype(BF16)
            turned[...] = turn(matrix[...])
            new_root[...] = dot(new_root[...], turned[...]).astype(BF16)
            return carry

        lax.fori_loop(1, steps, advance, 0)

    @pl.when(side == 0)
    def _():
        payload[...] = new_root[...]

    @pl.when(side != 0)
    def _():
        payload[...] = dot(grad[...], new_root[...]).astype(BF16)


def roots(info, own, last, other, other_last, state, stale):
    full = jax.ShapeDtypeStruct((BLOCK, BLOCK), BF16)
    return pl.pallas_call(
        newton_kernel,
        out_shape=(
            jax.ShapeDtypeStruct((BLOCK, BLOCK), F32),
            full,
            full,
            jax.ShapeDtypeStruct((1, 1), F32),
        ),
        in_specs=[SMEM] + [VMEM] * 6,
        out_specs=[VMEM] * 4,
        scratch_shapes=[pltpu.VMEM((BLOCK, BLOCK), BF16)] * 4,
        compiler_params=LIMIT,
    )(info, own, last, other, other_last, state, stale)


def update_kernel(info, own, other, grad_square, out):
    side = info[0]

    def finish(left, product, start):
        raw = dot(left[...], product[...])
        total = jnp.sum(raw * raw, keepdims=True)
        ratio = jnp.sqrt(grad_square[...]) / jnp.sqrt(total + NORM_EPS)
        out[...] = (raw[start : start + HALF] * ratio).astype(BF16)

    @pl.when(side == 0)
    def _():
        finish(own, other, 0)

    @pl.when(side != 0)
    def _():
        finish(other, own, HALF)


def grafted(info, own, other, grad_square):
    return pl.pallas_call(
        update_kernel,
        out_shape=jax.ShapeDtypeStruct((HALF, BLOCK), BF16),
        in_specs=[SMEM] + [VMEM] * 3,
        out_specs=VMEM,
        compiler_params=LIMIT,
    )(info, own, other, grad_square)


def other_of(value, axis):
    return lax.ppermute(value, axis, [(0, 1), (1, 0)])


def across_chip(value):
    return lax.ppermute(value, ("core", "y_hi"), [(i, 3 - i) for i in range(4)])


def along_z(value, by):
    size = lax.axis_size("z")
    return lax.ppermute(value, "z", [(i, (i - by) % size) for i in range(size)])


def two_away(value):
    size = lax.axis_size("z")
    pairs = [(i, (i - 2) % size) for i in range(size)]
    pairs += [(size + i, size + (i + 2) % size) for i in range(size)]
    return lax.ppermute(value, ("core", "z"), pairs)


def to_home(value):
    pairs = [(2 * lo + hi, 2 * hi + (hi ^ lo)) for lo in range(2) for hi in range(2)]
    return lax.ppermute(value, ("y_lo", "y_hi"), pairs)


def reduced(parts):
    got = lax.all_to_all(parts, ("y_lo", "x"), 0, 0, tiled=True)
    return jnp.sum(got.astype(F32), axis=0).astype(BF16)


def per_device(hidden, out_grad, token_counts, factor_state, stale_root, newton_steps):
    core = lax.axis_index("core")
    first = lax.rem(lax.axis_index("z"), CLASSES)
    positions = lax.broadcasted_iota(jnp.int32, (out_grad.shape[0], 1), 0)
    kept = jnp.where(positions < token_counts[0], out_grad, jnp.zeros_like(out_grad)).T
    rows = kept.shape[0] // 2
    mine = lax.dynamic_slice_in_dim(kept, core * rows, rows, 0)
    sent = lax.dynamic_slice_in_dim(kept, (1 - core) * rows, rows, 0)
    sent, hidden = lax.optimization_barrier((sent, hidden))
    block = jnp.concatenate([mine, other_of(sent, "core")], axis=1)
    far = other_of(hidden, "y_hi")
    near = other_of(hidden, "core")
    columns = (hidden, near, far, across_chip(hidden))
    size = lax.axis_size("z")
    strided = [[at + CLASSES * i for i in range(size // CLASSES)] for at in range(CLASSES)]
    own_class = lax.all_gather(block, "z", axis=0, tiled=True, axis_index_groups=strided)
    above = along_z(own_class, 1)
    below = along_z(own_class, -1)
    across = two_away(own_class)
    own = reduced(partials([own_class], columns))
    above, below, across, own = lax.optimization_barrier((above, below, across, own))
    rest = reduced(partials([above, below, across], columns))
    home = to_home(jnp.concatenate([own, rest], axis=0))
    away = other_of(home, "core")
    own, last, other, other_last = home[:192], home[192:], away[:192], away[192:]
    info = jnp.stack([core, first, newton_steps[0, 0]]).astype(jnp.int32)
    new_factor, new_root, payload, grad_square = roots(
        info, own, last, other, other_last, factor_state, stale_root
    )
    update = grafted(info, payload, other_of(payload, "core"), grad_square)
    return (update, new_factor, new_root)


def solution(mesh):
    fine = Mesh(mesh.devices.reshape(2, 4, 2, 2, 16), AXES)
    spec = P(AXES[:3], AXES[3:])
    in_specs = (spec, spec, P(AXES[:3]), spec, spec, spec)
    return jax.shard_map(per_device, mesh=fine, in_specs=in_specs, out_specs=(spec, spec, spec), check_vma=False)
```

```python
import functools

import jax
import jax.numpy as jnp
from jax import lax
from jax.experimental import pallas as pl
from jax.experimental.pallas import tpu as pltpu
from jax.sharding import Mesh
from jax.sharding import PartitionSpec as P

BETA = 0.9
NORM_EPS = 1e-06
BLOCK = 512
HALF = BLOCK // 2
CLASSES = 4
VMEM = pl.BlockSpec(memory_space=pltpu.VMEM)
SMEM = pl.BlockSpec(memory_space=pltpu.SMEM)
LIMIT = pltpu.CompilerParams(vmem_limit_bytes=48 * 2**20)
AXES = ("y_lo", "x", "core", "y_hi", "z")
BF16 = jnp.bfloat16
F32 = jnp.float32


def dot(a, b, contract=((1,), (0,))):
    return lax.dot_general(a, b, (contract, ((), ())), preferred_element_type=F32)


def total_of(value):
    return jnp.sum(jnp.sum(value, axis=0, keepdims=True), axis=1, keepdims=True)


def partial_kernel(classes, flip, *refs):
    features, hidden, out = refs[:classes], refs[classes:-1], refs[-1]
    rows = features[0].shape[0] // CLASSES
    for column in range(2):
        first = jnp.where(flip[0] == 0, column, 1 - column) * CLASSES
        for at in range(classes):
            total = dot(features[at][...], hidden[column][...]).astype(BF16)
            for block in range(CLASSES):
                out[first + block, at * rows : (at + 1) * rows, :] = total[
                    block * rows : (block + 1) * rows
                ]


def partials(flip, features, hidden):
    classes = len(features)
    rows = features[0].shape[0] // CLASSES
    width = hidden[0].shape[1]
    return pl.pallas_call(
        functools.partial(partial_kernel, classes),
        out_shape=jax.ShapeDtypeStruct((2 * CLASSES, classes * rows, width), BF16),
        in_specs=[SMEM] + [VMEM] * (classes + 2),
        out_specs=VMEM,
        compiler_params=LIMIT,
    )(flip, *features, *hidden)


def newton_kernel(info, own, last, other, other_last, state, stale, new_factor, new_root, payload, grad_square, grad, matrix, turned, square):
    side, first, steps = info[0], info[1], info[2]
    rows = HALF // CLASSES
    for at, shift in enumerate((0, 1, 3, 2)):
        start = lax.rem(first + shift, CLASSES) * (2 * rows)
        mine = pl.multiple_of(start + side * rows, rows)
        theirs = pl.multiple_of(start + (1 - side) * rows, rows)
        if at < CLASSES - 1:
            grad[pl.ds(mine, rows), :] = own[at * rows : (at + 1) * rows, :]
            grad[pl.ds(theirs, rows), :] = other[at * rows : (at + 1) * rows, :]
        else:
            grad[pl.ds(mine, rows), :] = last[...]
            grad[pl.ds(theirs, rows), :] = other_last[...]

    @pl.when(side == 0)
    def _():
        new_factor[...] = BETA * state[...] + (1.0 - BETA) * dot(grad[...], grad[...], ((1,), (1,)))

    @pl.when(side != 0)
    def _():
        new_factor[...] = BETA * state[...] + (1.0 - BETA) * dot(grad[...], grad[...], ((0,), (0,)))

    grad_square[...] = total_of(jnp.square(grad[...].astype(F32)))
    new_root[...] = stale[...]

    def turn(value):
        row = lax.broadcasted_iota(jnp.int32, value.shape, 0)
        column = lax.broadcasted_iota(jnp.int32, value.shape, 1)
        identity = jnp.where(row == column, 5.0, 0.0)
        return ((identity - value.astype(F32)) * 0.25).astype(BF16)

    @pl.when(steps > 0)
    def _():
        factor = new_factor[...]
        norm = jnp.sqrt(total_of(factor * factor) + NORM_EPS)
        matrix[...] = (factor * (1.0 / norm)).astype(BF16)
        root_scale = lax.rsqrt(jnp.sqrt(norm)).astype(BF16).astype(F32)
        turned[...] = turn(matrix[...])
        new_root[...] = (root_scale * turned[...].astype(F32)).astype(BF16)

        def advance(level, carry):
            square[...] = dot(turned[...], turned[...]).astype(BF16)
            square[...] = dot(square[...], square[...]).astype(BF16)
            matrix[...] = dot(square[...], matrix[...]).astype(BF16)
            turned[...] = turn(matrix[...])
            new_root[...] = dot(new_root[...], turned[...]).astype(BF16)
            return carry

        lax.fori_loop(1, steps, advance, 0)

    @pl.when(side == 0)
    def _():
        payload[...] = new_root[...]

    @pl.when(side != 0)
    def _():
        payload[...] = dot(grad[...], new_root[...]).astype(BF16)


def roots(info, own, last, other, other_last, state, stale):
    full = jax.ShapeDtypeStruct((BLOCK, BLOCK), BF16)
    return pl.pallas_call(
        newton_kernel,
        out_shape=(
            jax.ShapeDtypeStruct((BLOCK, BLOCK), F32),
            full,
            full,
            jax.ShapeDtypeStruct((1, 1), F32),
        ),
        in_specs=[SMEM] + [VMEM] * 6,
        out_specs=[VMEM] * 4,
        scratch_shapes=[pltpu.VMEM((BLOCK, BLOCK), BF16)] * 4,
        compiler_params=LIMIT,
    )(info, own, last, other, other_last, state, stale)


def update_kernel(info, own, other, grad_square, out):
    side = info[0]

    def finish(left, product, start):
        raw = dot(left[...], product[...])
        total = total_of(raw * raw)
        ratio = jnp.sqrt(grad_square[...]) / jnp.sqrt(total + NORM_EPS)
        out[...] = (raw[start : start + HALF] * ratio).astype(BF16)

    @pl.when(side == 0)
    def _():
        finish(own, other, 0)

    @pl.when(side != 0)
    def _():
        finish(other, own, HALF)


def grafted(info, own, other, grad_square):
    return pl.pallas_call(
        update_kernel,
        out_shape=jax.ShapeDtypeStruct((HALF, BLOCK), BF16),
        in_specs=[SMEM] + [VMEM] * 3,
        out_specs=VMEM,
        compiler_params=LIMIT,
    )(info, own, other, grad_square)


def other_of(value, axis):
    return lax.ppermute(value, axis, [(0, 1), (1, 0)])


def along_z(value, by):
    size = lax.axis_size("z")
    return lax.ppermute(value, "z", [(i, (i - by) % size) for i in range(size)])


def two_away(value):
    size = lax.axis_size("z")
    pairs = [(i, (i - 2) % size) for i in range(size)]
    pairs += [(size + i, size + (i + 2) % size) for i in range(size)]
    return lax.ppermute(value, ("core", "z"), pairs)


def to_home(value):
    pairs = [(2 * lo + hi, 2 * hi + lo) for lo in range(2) for hi in range(2)]
    return lax.ppermute(value, ("y_lo", "y_hi"), pairs)


def reduced(parts):
    got = lax.all_to_all(parts, ("y_lo", "x"), 0, 0, tiled=True)
    return jnp.sum(got.astype(F32), axis=0).astype(BF16)


def per_device(hidden, out_grad, token_counts, factor_state, stale_root, newton_steps):
    core = lax.axis_index("core")
    first = lax.rem(lax.axis_index("z"), CLASSES)
    column = jnp.concatenate([hidden, other_of(hidden, "core")], axis=0)
    columns = (column, other_of(column, "y_hi"))
    positions = lax.broadcasted_iota(jnp.int32, (out_grad.shape[0], 1), 0)
    kept = jnp.where(positions < token_counts[0], out_grad, jnp.zeros_like(out_grad)).T
    rows = kept.shape[0] // 2
    mine = lax.dynamic_slice_in_dim(kept, core * rows, rows, 0)
    sent = lax.dynamic_slice_in_dim(kept, (1 - core) * rows, rows, 0)
    block = jnp.concatenate([mine, other_of(sent, "core")], axis=1)
    size = lax.axis_size("z")
    strided = [[at + CLASSES * i for i in range(size // CLASSES)] for at in range(CLASSES)]
    own_class = lax.all_gather(block, "z", axis=0, tiled=True, axis_index_groups=strided)
    above = along_z(own_class, 1)
    below = along_z(own_class, -1)
    across = two_away(own_class)
    flip = lax.axis_index("y_hi").astype(jnp.int32).reshape(1)
    own = reduced(partials(flip, [own_class], columns))
    above, below, across, own = lax.optimization_barrier((above, below, across, own))
    rest = reduced(partials(flip, [above, below, across], columns))
    home = to_home(jnp.concatenate([own, rest], axis=0))
    away = other_of(home, "core")
    own, last, other, other_last = home[:192], home[192:], away[:192], away[192:]
    info = jnp.stack([core, first, newton_steps[0, 0]]).astype(jnp.int32)
    new_factor, new_root, payload, grad_square = roots(
        info, own, last, other, other_last, factor_state, stale_root
    )
    update = grafted(info, payload, other_of(payload, "core"), grad_square)
    return (update, new_factor, new_root)


def solution(mesh):
    fine = Mesh(mesh.devices.reshape(2, 4, 2, 2, 16), AXES)
    spec = P(AXES[:3], AXES[3:])
    in_specs = (spec, spec, P(AXES[:3]), spec, spec, spec)
    return jax.shard_map(per_device, mesh=fine, in_specs=in_specs, out_specs=(spec, spec, spec), check_vma=False)
```

```python
import functools

import jax
import jax.numpy as jnp
from jax import lax
from jax.experimental import pallas as pl
from jax.experimental.pallas import tpu as pltpu
from jax.sharding import Mesh
from jax.sharding import PartitionSpec as P

BETA = 0.9
NORM_EPS = 1e-06
BLOCK = 512
HALF = BLOCK // 2
CLASSES = 4
VMEM = pl.BlockSpec(memory_space=pltpu.VMEM)
SMEM = pl.BlockSpec(memory_space=pltpu.SMEM)
LIMIT = pltpu.CompilerParams(vmem_limit_bytes=16 * 2**20)
AXES = ("y_lo", "x", "core", "y_hi", "z")
BF16 = jnp.bfloat16
F32 = jnp.float32


def dot(a, b, contract=((1,), (0,))):
    return lax.dot_general(a, b, (contract, ((), ())), preferred_element_type=F32)


def total_of(value):
    return jnp.sum(jnp.sum(value, axis=0, keepdims=True), axis=1, keepdims=True)


def partial_kernel(classes, *refs):
    features, hidden, out = refs[:classes], refs[classes:-1], refs[-1]
    rows = features[0].shape[0] // CLASSES
    own = lax.axis_index("y_hi")
    for column in range(2):
        first = (own + column - 2 * own * column) * CLASSES
        for at in range(classes):
            total = dot(features[at][...], hidden[column][...]).astype(BF16)
            for block in range(CLASSES):
                out[first + block, at * rows : (at + 1) * rows, :] = total[
                    block * rows : (block + 1) * rows
                ]


def partials(features, hidden):
    classes = len(features)
    rows = features[0].shape[0] // CLASSES
    width = hidden[0].shape[1]
    return pl.pallas_call(
        functools.partial(partial_kernel, classes),
        out_shape=jax.ShapeDtypeStruct((2 * CLASSES, classes * rows, width), BF16),
        in_specs=[VMEM] * (classes + 2),
        out_specs=VMEM,
        compiler_params=LIMIT,
    )(*features, *hidden)


def newton_kernel(count, own, other, state, stale, new_factor, new_root, payload, grad_square, grad, matrix, turned, square):
    side, first, steps = lax.axis_index("core"), lax.rem(lax.axis_index("z"), CLASSES), count[0, 0]
    rows = HALF // CLASSES
    for at, shift in enumerate((0, 1, 3, 2)):
        start = lax.rem(first + shift, CLASSES) * (2 * rows)
        mine = pl.multiple_of(start + side * rows, rows)
        theirs = pl.multiple_of(start + (1 - side) * rows, rows)
        grad[pl.ds(mine, rows), :] = own[at * rows : (at + 1) * rows, :]
        grad[pl.ds(theirs, rows), :] = other[at * rows : (at + 1) * rows, :]

    @pl.when(side == 0)
    def _():
        new_factor[...] = BETA * state[...] + (1.0 - BETA) * dot(grad[...], grad[...], ((1,), (1,)))

    @pl.when(side != 0)
    def _():
        new_factor[...] = BETA * state[...] + (1.0 - BETA) * dot(grad[...], grad[...], ((0,), (0,)))

    grad_square[...] = jnp.broadcast_to(total_of(jnp.square(grad[...].astype(F32))), grad_square.shape)
    new_root[...] = stale[...]

    def turn(value):
        row = lax.broadcasted_iota(jnp.int32, value.shape, 0)
        column = lax.broadcasted_iota(jnp.int32, value.shape, 1)
        identity = jnp.where(row == column, 5.0, 0.0)
        return ((identity - value.astype(F32)) * 0.25).astype(BF16)

    @pl.when(steps > 0)
    def _():
        factor = new_factor[...]
        norm = jnp.sqrt(total_of(factor * factor) + NORM_EPS)
        matrix[...] = (factor * (1.0 / norm)).astype(BF16)
        root_scale = lax.rsqrt(jnp.sqrt(norm)).astype(BF16).astype(F32)
        turned[...] = turn(matrix[...])
        new_root[...] = (root_scale * turned[...].astype(F32)).astype(BF16)

        def advance(level, carry):
            square[...] = dot(turned[...], turned[...]).astype(BF16)
            square[...] = dot(square[...], square[...]).astype(BF16)
            matrix[...] = dot(square[...], matrix[...]).astype(BF16)
            turned[...] = turn(matrix[...])
            new_root[...] = dot(new_root[...], turned[...]).astype(BF16)
            return carry

        lax.fori_loop(1, steps, advance, 0)

    @pl.when(side == 0)
    def _():
        payload[...] = new_root[...]

    @pl.when(side != 0)
    def _():
        payload[...] = dot(grad[...], new_root[...]).astype(BF16)


def roots(count, own, other, state, stale):
    full = jax.ShapeDtypeStruct((BLOCK, BLOCK), BF16)
    return pl.pallas_call(
        newton_kernel,
        out_shape=(
            jax.ShapeDtypeStruct((BLOCK, BLOCK), F32),
            full,
            full,
            jax.ShapeDtypeStruct((8, 128), F32),
        ),
        in_specs=[SMEM] + [VMEM] * 4,
        out_specs=[VMEM] * 4,
        scratch_shapes=[pltpu.VMEM((BLOCK, BLOCK), BF16)] * 4,
        compiler_params=LIMIT,
    )(count, own, other, state, stale)


def update_kernel(own, other, grad_square, out):
    side = lax.axis_index("core")

    def finish(left, product, start):
        raw = dot(left[...], product[...])
        total = total_of(raw * raw)
        ratio = jnp.sqrt(grad_square[:1, :1]) / jnp.sqrt(total + NORM_EPS)
        out[...] = (raw[start : start + HALF] * ratio).astype(BF16)

    @pl.when(side == 0)
    def _():
        finish(own, other, 0)

    @pl.when(side != 0)
    def _():
        finish(other, own, HALF)


def grafted(own, other, grad_square):
    return pl.pallas_call(
        update_kernel,
        out_shape=jax.ShapeDtypeStruct((HALF, BLOCK), BF16),
        in_specs=[VMEM] * 3,
        out_specs=VMEM,
        compiler_params=LIMIT,
    )(own, other, grad_square)


def other_of(value, axis):
    return lax.ppermute(value, axis, [(0, 1), (1, 0)])


def along_z(value, by):
    size = lax.axis_size("z")
    return lax.ppermute(value, "z", [(i, (i - by) % size) for i in range(size)])


def two_away(value):
    size = lax.axis_size("z")
    pairs = [(i, (i - 2) % size) for i in range(size)]
    pairs += [(size + i, size + (i + 2) % size) for i in range(size)]
    return lax.ppermute(value, ("core", "z"), pairs)


def to_home(value):
    pairs = [(2 * lo + hi, 2 * hi + lo) for lo in range(2) for hi in range(2)]
    return lax.ppermute(value, ("y_lo", "y_hi"), pairs)


def reduced(parts):
    got = lax.all_to_all(parts, ("y_lo", "x"), 0, 0, tiled=True)
    return jnp.sum(got.astype(F32), axis=0).astype(BF16)


def per_device(hidden, out_grad, token_counts, factor_state, stale_root, newton_steps):
    core = lax.axis_index("core")
    column = jnp.concatenate([hidden, other_of(hidden, "core")], axis=0)
    columns = (column, other_of(column, "y_hi"))
    positions = lax.broadcasted_iota(jnp.int32, (out_grad.shape[0], 1), 0)
    kept = jnp.where(positions < token_counts[0], out_grad, jnp.zeros_like(out_grad)).T
    rows = kept.shape[0] // 2
    mine = lax.dynamic_slice_in_dim(kept, core * rows, rows, 0)
    sent = lax.dynamic_slice_in_dim(kept, (1 - core) * rows, rows, 0)
    block = jnp.concatenate([mine, other_of(sent, "core")], axis=1)
    size = lax.axis_size("z")
    strided = [[at + CLASSES * i for i in range(size // CLASSES)] for at in range(CLASSES)]
    own_class = lax.all_gather(block, "z", axis=0, tiled=True, axis_index_groups=strided)
    above = along_z(own_class, 1)
    below = along_z(own_class, -1)
    across = two_away(own_class)
    own = reduced(partials([own_class], columns))
    above, below, across, own = lax.optimization_barrier((above, below, across, own))
    rest = reduced(partials([above, below, across], columns))
    own = to_home(jnp.concatenate([own, rest], axis=0))
    other = other_of(own, "core")
    new_factor, new_root, payload, grad_square = roots(newton_steps, own, other, factor_state, stale_root)
    update = grafted(payload, other_of(payload, "core"), grad_square)
    return (update, new_factor, new_root)


def solution(mesh):
    fine = Mesh(mesh.devices.reshape(2, 4, 2, 2, 16), AXES)
    spec = P(AXES[:3], AXES[3:])
    in_specs = (spec, spec, P(AXES[:3]), spec, spec, spec)
    return jax.shard_map(per_device, mesh=fine, in_specs=in_specs, out_specs=(spec, spec, spec), check_vma=False)
```

```python
import functools

import jax
import jax.numpy as jnp
from jax import lax
from jax.experimental import pallas as pl
from jax.experimental.pallas import tpu as pltpu
from jax.sharding import Mesh
from jax.sharding import PartitionSpec as P

BETA = 0.9
NORM_EPS = 1e-06
BLOCK = 512
HALF = BLOCK // 2
CLASSES = 4
VMEM = pl.BlockSpec(memory_space=pltpu.VMEM)
SMEM = pl.BlockSpec(memory_space=pltpu.SMEM)
LIMIT = pltpu.CompilerParams(vmem_limit_bytes=16 * 2**20)
AXES = ("y_lo", "x", "core", "y_hi", "z")
BF16 = jnp.bfloat16
F32 = jnp.float32


def dot(a, b, contract=((1,), (0,))):
    return lax.dot_general(a, b, (contract, ((), ())), preferred_element_type=F32)


def total_of(value):
    return jnp.sum(jnp.sum(value, axis=0, keepdims=True), axis=1, keepdims=True)


def partial_kernel(classes, *refs):
    features, hidden, out, held, sems = refs[:classes], refs[classes:-3], refs[-3], refs[-2], refs[-1]
    rows = features[0].shape[0] // CLASSES
    own = lax.axis_index("y_hi")
    copies = [pltpu.make_async_copy(features[at], held.at[at], sems.at[at]) for at in range(classes)]
    for copy in copies:
        copy.start()
    for at in range(classes):
        copies[at].wait()
        for column in range(2):
            first = (own + column - 2 * own * column) * CLASSES
            total = dot(held[at], hidden[column][...]).astype(BF16)
            for block in range(CLASSES):
                out[first + block, at * rows : (at + 1) * rows, :] = total[
                    block * rows : (block + 1) * rows
                ]


def partials(features, hidden):
    classes = len(features)
    height, tokens = features[0].shape
    rows = height // CLASSES
    width = hidden[0].shape[1]
    return pl.pallas_call(
        functools.partial(partial_kernel, classes),
        out_shape=jax.ShapeDtypeStruct((2 * CLASSES, classes * rows, width), BF16),
        in_specs=[pl.BlockSpec(memory_space=pl.ANY)] * classes + [VMEM] * 2,
        out_specs=VMEM,
        scratch_shapes=[pltpu.VMEM((classes, height, tokens), BF16), pltpu.SemaphoreType.DMA((classes,))],
        compiler_params=LIMIT,
    )(*features, *hidden)


def newton_kernel(count, own, other, state, stale, new_factor, new_root, payload, grad_square, grad, matrix, turned, square):
    side, first, steps = lax.axis_index("core"), lax.rem(lax.axis_index("z"), CLASSES), count[0, 0]
    rows = HALF // CLASSES
    for at, shift in enumerate((0, 1, 3, 2)):
        start = lax.rem(first + shift, CLASSES) * (2 * rows)
        mine = pl.multiple_of(start + side * rows, rows)
        theirs = pl.multiple_of(start + (1 - side) * rows, rows)
        grad[pl.ds(mine, rows), :] = own[at * rows : (at + 1) * rows, :]
        grad[pl.ds(theirs, rows), :] = other[at * rows : (at + 1) * rows, :]

    @pl.when(side == 0)
    def _():
        new_factor[...] = BETA * state[...] + (1.0 - BETA) * dot(grad[...], grad[...], ((1,), (1,)))

    @pl.when(side != 0)
    def _():
        new_factor[...] = BETA * state[...] + (1.0 - BETA) * dot(grad[...], grad[...], ((0,), (0,)))

    grad_square[...] = jnp.broadcast_to(total_of(jnp.square(grad[...].astype(F32))), grad_square.shape)
    new_root[...] = stale[...]

    def turn(value):
        row = lax.broadcasted_iota(jnp.int32, value.shape, 0)
        column = lax.broadcasted_iota(jnp.int32, value.shape, 1)
        identity = jnp.where(row == column, 5.0, 0.0)
        return ((identity - value.astype(F32)) * 0.25).astype(BF16)

    @pl.when(steps > 0)
    def _():
        factor = new_factor[...]
        norm = jnp.sqrt(total_of(factor * factor) + NORM_EPS)
        matrix[...] = (factor * (1.0 / norm)).astype(BF16)
        root_scale = lax.rsqrt(jnp.sqrt(norm)).astype(BF16).astype(F32)
        turned[...] = turn(matrix[...])
        new_root[...] = (root_scale * turned[...].astype(F32)).astype(BF16)

        def advance(level, carry):
            square[...] = dot(turned[...], turned[...]).astype(BF16)
            square[...] = dot(square[...], square[...]).astype(BF16)
            matrix[...] = dot(square[...], matrix[...]).astype(BF16)
            turned[...] = turn(matrix[...])
            new_root[...] = dot(new_root[...], turned[...]).astype(BF16)
            return carry

        lax.fori_loop(1, steps, advance, 0)

    @pl.when(side == 0)
    def _():
        payload[...] = new_root[...]

    @pl.when(side != 0)
    def _():
        payload[...] = dot(grad[...], new_root[...]).astype(BF16)


def roots(count, own, other, state, stale):
    full = jax.ShapeDtypeStruct((BLOCK, BLOCK), BF16)
    return pl.pallas_call(
        newton_kernel,
        out_shape=(
            jax.ShapeDtypeStruct((BLOCK, BLOCK), F32),
            full,
            full,
            jax.ShapeDtypeStruct((8, 128), F32),
        ),
        in_specs=[SMEM] + [VMEM] * 4,
        out_specs=[VMEM] * 4,
        scratch_shapes=[pltpu.VMEM((BLOCK, BLOCK), BF16)] * 4,
        compiler_params=LIMIT,
    )(count, own, other, state, stale)


def update_kernel(own, other, grad_square, out):
    side = lax.axis_index("core")

    def finish(left, product, start):
        raw = dot(left[...], product[...])
        total = total_of(raw * raw)
        ratio = jnp.sqrt(grad_square[:1, :1]) / jnp.sqrt(total + NORM_EPS)
        out[...] = (raw[start : start + HALF] * ratio).astype(BF16)

    @pl.when(side == 0)
    def _():
        finish(own, other, 0)

    @pl.when(side != 0)
    def _():
        finish(other, own, HALF)


def grafted(own, other, grad_square):
    return pl.pallas_call(
        update_kernel,
        out_shape=jax.ShapeDtypeStruct((HALF, BLOCK), BF16),
        in_specs=[VMEM] * 3,
        out_specs=VMEM,
        compiler_params=LIMIT,
    )(own, other, grad_square)


def other_of(value, axis):
    return lax.ppermute(value, axis, [(0, 1), (1, 0)])


def along_z(value, by):
    size = lax.axis_size("z")
    return lax.ppermute(value, "z", [(i, (i - by) % size) for i in range(size)])


def two_away(value):
    size = lax.axis_size("z")
    pairs = [(i, (i - 2) % size) for i in range(size)]
    pairs += [(size + i, size + (i + 2) % size) for i in range(size)]
    return lax.ppermute(value, ("core", "z"), pairs)


def to_home(value):
    pairs = [(2 * lo + hi, 2 * hi + lo) for lo in range(2) for hi in range(2)]
    return lax.ppermute(value, ("y_lo", "y_hi"), pairs)


def reduced(parts):
    got = lax.all_to_all(parts, ("y_lo", "x"), 0, 0, tiled=True)
    return jnp.sum(got.astype(F32), axis=0).astype(BF16)


def per_device(hidden, out_grad, token_counts, factor_state, stale_root, newton_steps):
    core = lax.axis_index("core")
    column = jnp.concatenate([hidden, other_of(hidden, "core")], axis=0)
    columns = (column, other_of(column, "y_hi"))
    positions = lax.broadcasted_iota(jnp.int32, (out_grad.shape[0], 1), 0)
    kept = jnp.where(positions < token_counts[0], out_grad, jnp.zeros_like(out_grad)).T
    rows = kept.shape[0] // 2
    mine = lax.dynamic_slice_in_dim(kept, core * rows, rows, 0)
    sent = lax.dynamic_slice_in_dim(kept, (1 - core) * rows, rows, 0)
    block = jnp.concatenate([mine, other_of(sent, "core")], axis=1)
    size = lax.axis_size("z")
    strided = [[at + CLASSES * i for i in range(size // CLASSES)] for at in range(CLASSES)]
    own_class = lax.all_gather(block, "z", axis=0, tiled=True, axis_index_groups=strided)
    above = along_z(own_class, 1)
    below = along_z(own_class, -1)
    across = two_away(own_class)
    own = reduced(partials([own_class], columns))
    above, below, across, own = lax.optimization_barrier((above, below, across, own))
    rest = reduced(partials([above, below, across], columns))
    own = to_home(jnp.concatenate([own, rest], axis=0))
    other = other_of(own, "core")
    new_factor, new_root, payload, grad_square = roots(newton_steps, own, other, factor_state, stale_root)
    update = grafted(payload, other_of(payload, "core"), grad_square)
    return (update, new_factor, new_root)


def solution(mesh):
    fine = Mesh(mesh.devices.reshape(2, 4, 2, 2, 16), AXES)
    spec = P(AXES[:3], AXES[3:])
    in_specs = (spec, spec, P(AXES[:3]), spec, spec, spec)
    return jax.shard_map(per_device, mesh=fine, in_specs=in_specs, out_specs=(spec, spec, spec), check_vma=False)
```

```python
import functools

import jax
import jax.numpy as jnp
from jax import lax
from jax.experimental import pallas as pl
from jax.experimental.pallas import tpu as pltpu
from jax.sharding import Mesh
from jax.sharding import PartitionSpec as P

BETA = 0.9
NORM_EPS = 1e-06
BLOCK = 512
HALF = BLOCK // 2
CLASSES = 4
VMEM = pl.BlockSpec(memory_space=pltpu.VMEM)
SMEM = pl.BlockSpec(memory_space=pltpu.SMEM)
LIMIT = pltpu.CompilerParams(vmem_limit_bytes=16 * 2**20)
AXES = ("y_lo", "x", "core", "y_hi", "z")
BF16 = jnp.bfloat16
F32 = jnp.float32


def dot(a, b, contract=((1,), (0,))):
    return lax.dot_general(a, b, (contract, ((), ())), preferred_element_type=F32)


def total_of(value):
    return jnp.sum(jnp.sum(value, axis=0, keepdims=True), axis=1, keepdims=True)


def partial_kernel(classes, *refs):
    features, hidden, out, held, sems = refs[:classes], refs[classes:-3], refs[-3], refs[-2], refs[-1]
    rows = features[0].shape[0] // CLASSES
    own = lax.axis_index("y_hi")
    copies = [pltpu.make_async_copy(features[at], held.at[at], sems.at[at]) for at in range(classes)]
    for copy in copies:
        copy.start()
    for at in range(classes):
        copies[at].wait()
        for column in range(2):
            first = (own + column - 2 * own * column) * CLASSES
            total = dot(held[at], hidden[column][...]).astype(BF16)
            for block in range(CLASSES):
                out[first + block, at * rows : (at + 1) * rows, :] = total[
                    block * rows : (block + 1) * rows
                ]


def partials(features, hidden):
    classes = len(features)
    height, tokens = features[0].shape
    rows = height // CLASSES
    width = hidden[0].shape[1]
    return pl.pallas_call(
        functools.partial(partial_kernel, classes),
        out_shape=jax.ShapeDtypeStruct((2 * CLASSES, classes * rows, width), BF16),
        in_specs=[pl.BlockSpec(memory_space=pl.ANY)] * classes + [VMEM] * 2,
        out_specs=VMEM,
        scratch_shapes=[pltpu.VMEM((classes, height, tokens), BF16), pltpu.SemaphoreType.DMA((classes,))],
        compiler_params=LIMIT,
    )(*features, *hidden)


def newton_kernel(count, own, other, state, stale, new_factor, new_root, payload, grad_square, grad, matrix, turned, square):
    side, first, steps = lax.axis_index("core"), lax.rem(lax.axis_index("z"), CLASSES), count[0, 0]
    rows = HALF // CLASSES
    for at, shift in enumerate((0, 2, 1, 3)):
        start = lax.rem(first + shift, CLASSES) * (2 * rows)
        mine = pl.multiple_of(start + side * rows, rows)
        theirs = pl.multiple_of(start + (1 - side) * rows, rows)
        grad[pl.ds(mine, rows), :] = own[at * rows : (at + 1) * rows, :]
        grad[pl.ds(theirs, rows), :] = other[at * rows : (at + 1) * rows, :]

    @pl.when(side == 0)
    def _():
        new_factor[...] = BETA * state[...] + (1.0 - BETA) * dot(grad[...], grad[...], ((1,), (1,)))

    @pl.when(side != 0)
    def _():
        new_factor[...] = BETA * state[...] + (1.0 - BETA) * dot(grad[...], grad[...], ((0,), (0,)))

    grad_square[...] = jnp.broadcast_to(total_of(jnp.square(grad[...].astype(F32))), grad_square.shape)
    new_root[...] = stale[...]

    def turn(value):
        row = lax.broadcasted_iota(jnp.int32, value.shape, 0)
        column = lax.broadcasted_iota(jnp.int32, value.shape, 1)
        identity = jnp.where(row == column, 5.0, 0.0)
        return ((identity - value.astype(F32)) * 0.25).astype(BF16)

    @pl.when(steps > 0)
    def _():
        factor = new_factor[...]
        norm = jnp.sqrt(total_of(factor * factor) + NORM_EPS)
        matrix[...] = (factor * (1.0 / norm)).astype(BF16)
        root_scale = lax.rsqrt(jnp.sqrt(norm)).astype(BF16).astype(F32)
        turned[...] = turn(matrix[...])
        new_root[...] = (root_scale * turned[...].astype(F32)).astype(BF16)

        def advance(level, carry):
            square[...] = dot(turned[...], turned[...]).astype(BF16)
            square[...] = dot(square[...], square[...]).astype(BF16)
            matrix[...] = dot(square[...], matrix[...]).astype(BF16)
            turned[...] = turn(matrix[...])
            new_root[...] = dot(new_root[...], turned[...]).astype(BF16)
            return carry

        lax.fori_loop(1, steps, advance, 0)

    @pl.when(side == 0)
    def _():
        payload[...] = new_root[...]

    @pl.when(side != 0)
    def _():
        payload[...] = dot(grad[...], new_root[...]).astype(BF16)


def roots(count, own, other, state, stale):
    full = jax.ShapeDtypeStruct((BLOCK, BLOCK), BF16)
    return pl.pallas_call(
        newton_kernel,
        out_shape=(
            jax.ShapeDtypeStruct((BLOCK, BLOCK), F32),
            full,
            full,
            jax.ShapeDtypeStruct((8, 128), F32),
        ),
        in_specs=[SMEM] + [VMEM] * 4,
        out_specs=[VMEM] * 4,
        scratch_shapes=[pltpu.VMEM((BLOCK, BLOCK), BF16)] * 4,
        compiler_params=LIMIT,
    )(count, own, other, state, stale)


def update_kernel(own, other, grad_square, out):
    side = lax.axis_index("core")

    def finish(left, product, start):
        raw = dot(left[...], product[...])
        total = total_of(raw * raw)
        ratio = jnp.sqrt(grad_square[:1, :1]) / jnp.sqrt(total + NORM_EPS)
        out[...] = (raw[start : start + HALF] * ratio).astype(BF16)

    @pl.when(side == 0)
    def _():
        finish(own, other, 0)

    @pl.when(side != 0)
    def _():
        finish(other, own, HALF)


def grafted(own, other, grad_square):
    return pl.pallas_call(
        update_kernel,
        out_shape=jax.ShapeDtypeStruct((HALF, BLOCK), BF16),
        in_specs=[VMEM] * 3,
        out_specs=VMEM,
        compiler_params=LIMIT,
    )(own, other, grad_square)


def other_of(value, axis):
    return lax.ppermute(value, axis, [(0, 1), (1, 0)])


def along_z(value, by):
    size = lax.axis_size("z")
    return lax.ppermute(value, "z", [(i, (i - by) % size) for i in range(size)])


def two_away(value):
    size = lax.axis_size("z")
    pairs = [(i, (i - 2) % size) for i in range(size)]
    pairs += [(size + i, size + (i + 2) % size) for i in range(size)]
    return lax.ppermute(value, ("core", "z"), pairs)


def to_home(value):
    pairs = [(2 * lo + hi, 2 * hi + lo) for lo in range(2) for hi in range(2)]
    return lax.ppermute(value, ("y_lo", "y_hi"), pairs)


def reduced(parts):
    got = lax.all_to_all(parts, ("y_lo", "x"), 0, 0, tiled=True)
    return jnp.sum(got.astype(F32), axis=0).astype(BF16)


def per_device(hidden, out_grad, token_counts, factor_state, stale_root, newton_steps):
    core = lax.axis_index("core")
    column = jnp.concatenate([hidden, other_of(hidden, "core")], axis=0)
    columns = (column, other_of(column, "y_hi"))
    positions = lax.broadcasted_iota(jnp.int32, (out_grad.shape[0], 1), 0)
    kept = jnp.where(positions < token_counts[0], out_grad, jnp.zeros_like(out_grad)).T
    rows = kept.shape[0] // 2
    mine = lax.dynamic_slice_in_dim(kept, core * rows, rows, 0)
    sent = lax.dynamic_slice_in_dim(kept, (1 - core) * rows, rows, 0)
    block = jnp.concatenate([mine, other_of(sent, "core")], axis=1)
    size = lax.axis_size("z")
    strided = [[at + CLASSES * i for i in range(size // CLASSES)] for at in range(CLASSES)]
    own_class = lax.all_gather(block, "z", axis=0, tiled=True, axis_index_groups=strided)
    across = two_away(own_class)
    above = along_z(own_class, 1)
    below = along_z(own_class, -1)
    own = reduced(partials([own_class], columns))
    across, above, below, own = lax.optimization_barrier((across, above, below, own))
    rest = reduced(partials([across, above, below], columns))
    own = to_home(jnp.concatenate([own, rest], axis=0))
    other = other_of(own, "core")
    new_factor, new_root, payload, grad_square = roots(newton_steps, own, other, factor_state, stale_root)
    update = grafted(payload, other_of(payload, "core"), grad_square)
    return (update, new_factor, new_root)


def solution(mesh):
    fine = Mesh(mesh.devices.reshape(2, 4, 2, 2, 16), AXES)
    spec = P(AXES[:3], AXES[3:])
    in_specs = (spec, spec, P(AXES[:3]), spec, spec, spec)
    return jax.shard_map(per_device, mesh=fine, in_specs=in_specs, out_specs=(spec, spec, spec), check_vma=False)
```

```python
import functools

import jax
import jax.numpy as jnp
from jax import lax
from jax.experimental import pallas as pl
from jax.experimental.pallas import tpu as pltpu
from jax.sharding import Mesh
from jax.sharding import PartitionSpec as P

BETA = 0.9
NORM_EPS = 1e-06
BLOCK = 512
HALF = BLOCK // 2
CLASSES = 4
VMEM = pl.BlockSpec(memory_space=pltpu.VMEM)
SMEM = pl.BlockSpec(memory_space=pltpu.SMEM)
LIMIT = pltpu.CompilerParams(vmem_limit_bytes=16 * 2**20)
AXES = ("y_lo", "x", "core", "y_hi", "z")
BF16 = jnp.bfloat16
F32 = jnp.float32


def dot(a, b, contract=((1,), (0,))):
    return lax.dot_general(a, b, (contract, ((), ())), preferred_element_type=F32)


def total_of(value):
    return jnp.sum(jnp.sum(value, axis=0, keepdims=True), axis=1, keepdims=True)


def partial_kernel(classes, *refs):
    features, hidden, out, held, sems = refs[:classes], refs[classes:-3], refs[-3], refs[-2], refs[-1]
    rows = features[0].shape[0] // CLASSES
    own = lax.axis_index("y_hi")
    copies = [pltpu.make_async_copy(features[at], held.at[at], sems.at[at]) for at in range(classes)]
    for copy in copies:
        copy.start()
    for at in range(classes):
        copies[at].wait()
        for column in range(2):
            first = (own + column - 2 * own * column) * CLASSES
            total = dot(held[at], hidden[column][...]).astype(BF16)
            for block in range(CLASSES):
                out[first + block, at * rows : (at + 1) * rows, :] = total[
                    block * rows : (block + 1) * rows
                ]


def partials(features, hidden):
    classes = len(features)
    height, tokens = features[0].shape
    rows = height // CLASSES
    width = hidden[0].shape[1]
    return pl.pallas_call(
        functools.partial(partial_kernel, classes),
        out_shape=jax.ShapeDtypeStruct((2 * CLASSES, classes * rows, width), BF16),
        in_specs=[pl.BlockSpec(memory_space=pl.ANY)] * classes + [VMEM] * 2,
        out_specs=VMEM,
        scratch_shapes=[pltpu.VMEM((classes, height, tokens), BF16), pltpu.SemaphoreType.DMA((classes,))],
        compiler_params=LIMIT,
    )(*features, *hidden)


def newton_kernel(count, own, other, state, stale, new_factor, new_root, payload, grad_square, grad, matrix, turned, square):
    side, first, steps = lax.axis_index("core"), lax.rem(lax.axis_index("z"), CLASSES), count[0, 0]
    rows = HALF // CLASSES
    for at, shift in enumerate((0, 2, 1, 3)):
        start = lax.rem(first + shift, CLASSES) * (2 * rows)
        mine = pl.multiple_of(start + side * rows, rows)
        theirs = pl.multiple_of(start + (1 - side) * rows, rows)
        grad[pl.ds(mine, rows), :] = own[at * rows : (at + 1) * rows, :]
        grad[pl.ds(theirs, rows), :] = other[at * rows : (at + 1) * rows, :]

    @pl.when(side == 0)
    def _():
        new_factor[...] = BETA * state[...] + (1.0 - BETA) * dot(grad[...], grad[...], ((1,), (1,)))

    @pl.when(side != 0)
    def _():
        new_factor[...] = BETA * state[...] + (1.0 - BETA) * dot(grad[...], grad[...], ((0,), (0,)))

    grad_square[...] = jnp.broadcast_to(total_of(jnp.square(grad[...].astype(F32))), grad_square.shape)
    new_root[...] = stale[...]

    def turn(value):
        row = lax.broadcasted_iota(jnp.int32, value.shape, 0)
        column = lax.broadcasted_iota(jnp.int32, value.shape, 1)
        identity = jnp.where(row == column, 5.0, 0.0)
        return ((identity - value.astype(F32)) * 0.25).astype(BF16)

    @pl.when(steps > 0)
    def _():
        factor = new_factor[...]
        norm = jnp.sqrt(total_of(factor * factor) + NORM_EPS)
        matrix[...] = (factor * (1.0 / norm)).astype(BF16)
        root_scale = lax.rsqrt(jnp.sqrt(norm)).astype(BF16).astype(F32)
        turned[...] = turn(matrix[...])
        new_root[...] = (root_scale * turned[...].astype(F32)).astype(BF16)

        def advance(level, carry):
            square[...] = dot(turned[...], turned[...]).astype(BF16)
            square[...] = dot(square[...], square[...]).astype(BF16)
            matrix[...] = dot(square[...], matrix[...]).astype(BF16)
            turned[...] = turn(matrix[...])
            new_root[...] = dot(new_root[...], turned[...]).astype(BF16)
            return carry

        lax.fori_loop(1, steps, advance, 0)

    @pl.when(side == 0)
    def _():
        payload[...] = new_root[...]

    @pl.when(side != 0)
    def _():
        payload[...] = dot(grad[...], new_root[...]).astype(BF16)


def roots(count, own, other, state, stale):
    full = jax.ShapeDtypeStruct((BLOCK, BLOCK), BF16)
    return pl.pallas_call(
        newton_kernel,
        out_shape=(
            jax.ShapeDtypeStruct((BLOCK, BLOCK), F32),
            full,
            full,
            jax.ShapeDtypeStruct((8, 128), F32),
        ),
        in_specs=[SMEM] + [VMEM] * 4,
        out_specs=[VMEM] * 4,
        scratch_shapes=[pltpu.VMEM((BLOCK, BLOCK), BF16)] * 4,
        compiler_params=LIMIT,
    )(count, own, other, state, stale)


def update_kernel(own, other, grad_square, out):
    side = lax.axis_index("core")

    def finish(left, product, start):
        raw = dot(left[...], product[...])
        total = total_of(raw * raw)
        ratio = jnp.sqrt(grad_square[:1, :1]) / jnp.sqrt(total + NORM_EPS)
        out[...] = (raw[start : start + HALF] * ratio).astype(BF16)

    @pl.when(side == 0)
    def _():
        finish(own, other, 0)

    @pl.when(side != 0)
    def _():
        finish(other, own, HALF)


def grafted(own, other, grad_square):
    return pl.pallas_call(
        update_kernel,
        out_shape=jax.ShapeDtypeStruct((HALF, BLOCK), BF16),
        in_specs=[VMEM] * 3,
        out_specs=VMEM,
        compiler_params=LIMIT,
    )(own, other, grad_square)


def other_of(value, axis):
    return lax.ppermute(value, axis, [(0, 1), (1, 0)])


def along_z(value, by):
    size = lax.axis_size("z")
    return lax.ppermute(value, "z", [(i, (i - by) % size) for i in range(size)])


def two_away(value):
    size = lax.axis_size("z")
    pairs = [(i, (i - 2) % size) for i in range(size)]
    pairs += [(size + i, size + (i + 2) % size) for i in range(size)]
    return lax.ppermute(value, ("core", "z"), pairs)


def to_home(value):
    pairs = [(2 * lo + hi, 2 * hi + lo) for lo in range(2) for hi in range(2)]
    return lax.ppermute(value, ("y_lo", "y_hi"), pairs)


def reduced(parts):
    got = lax.all_to_all(parts, ("y_lo", "x"), 0, 0, tiled=True)
    return jnp.sum(got.astype(F32), axis=0).astype(BF16)


def per_device(hidden, out_grad, token_counts, factor_state, stale_root, newton_steps):
    core = lax.axis_index("core")
    column = jnp.concatenate([hidden, other_of(hidden, "core")], axis=0)
    positions = lax.broadcasted_iota(jnp.int32, (out_grad.shape[0], 1), 0)
    kept = jnp.where(positions < token_counts[0], out_grad, jnp.zeros_like(out_grad)).T
    rows = kept.shape[0] // 2
    mine = lax.dynamic_slice_in_dim(kept, core * rows, rows, 0)
    sent = lax.dynamic_slice_in_dim(kept, (1 - core) * rows, rows, 0)
    got, column = lax.optimization_barrier((other_of(sent, "core"), column))
    columns = (column, other_of(column, "y_hi"))
    block = jnp.concatenate([mine, got], axis=1)
    size = lax.axis_size("z")
    strided = [[at + CLASSES * i for i in range(size // CLASSES)] for at in range(CLASSES)]
    own_class = lax.all_gather(block, "z", axis=0, tiled=True, axis_index_groups=strided)
    across = two_away(own_class)
    above = along_z(own_class, 1)
    below = along_z(own_class, -1)
    own = reduced(partials([own_class], columns))
    across, above, below, own = lax.optimization_barrier((across, above, below, own))
    rest = reduced(partials([across, above, below], columns))
    own = to_home(jnp.concatenate([own, rest], axis=0))
    other = other_of(own, "core")
    new_factor, new_root, payload, grad_square = roots(newton_steps, own, other, factor_state, stale_root)
    update = grafted(payload, other_of(payload, "core"), grad_square)
    return (update, new_factor, new_root)


def solution(mesh):
    fine = Mesh(mesh.devices.reshape(2, 4, 2, 2, 16), AXES)
    spec = P(AXES[:3], AXES[3:])
    in_specs = (spec, spec, P(AXES[:3]), spec, spec, spec)
    return jax.shard_map(per_device, mesh=fine, in_specs=in_specs, out_specs=(spec, spec, spec), check_vma=False)
```
